32 devices in a mesh: grp: 2 (over y), blk: 4 (over z), col: 2 (over x), rhs: 2 (over core).
Axes of the slice: x: 2, y: 2, z: 4, core: 2. Of those that a mesh axis runs over, the one named last changes fastest.
Arguments:
- vector: bfloat16 [8192, 256], P(('grp', 'blk'), 'rhs'), parts along dimension 0, may hold values from -24 to 24
- self_term: float32 [8192], P(('grp', 'blk')), parts along dimension 0, may hold values from 1 to 4
- near_blocks: bfloat16 [480, 256, 256], P(('grp', 'blk', 'col')), parts along dimension 0, may hold values from -0.09375 to 0.09375
- near_rows: int32 [480], P(('grp', 'blk', 'col')), parts along dimension 0, may hold values from 0 to 3
- near_source: int32 [480], P(('grp', 'blk', 'col')), parts along dimension 0, may hold values from 0 to 7, as said below
- send_index: int32 [8, 4], P(('grp', 'blk')), parts along dimension 0, may hold values from 0 to 4, as said below
- source_basis: bfloat16 [32, 32, 256], P(('grp', 'blk')), parts along dimension 0, may hold values from -0.375 to 0.375
- target_basis: bfloat16 [32, 32, 256], P(('grp', 'blk')), parts along dimension 0, may hold values from -1 to 1
- couplings: bfloat16 [1024, 32, 32], P(('grp', 'blk', 'col')), parts along dimension 0, may hold values from -0.1875 to 0.1875
- far_rows: int32 [1024], P(('grp', 'blk', 'col')), parts along dimension 0, may hold values from 0 to 3
- far_cols: int32 [1024], P(('grp', 'blk', 'col')), parts along dimension 0, may hold values from 0 to 15
Outputs:
- last_vector: bfloat16 [8192, 256], P(('grp', 'blk', 'col'), 'rhs'), parts along dimension 0
- hessenberg: float32 [18, 256], P('grp', 'rhs'), parts along dimension 0
The draws below stay inside these ranges and needn't reach their ends.
There are 2 independent parts, one for each index of `grp`. The reference program is written for one: setup_inputs(seed, part) draws one part's arguments, and reference() takes and returns one part's arrays. A program takes and returns all parts, laid end to end along the dimension named above; each array names one. Nothing has to cross between parts.
Inputs may be any that keep to these rules, and one draw needn't show every extreme that they name: send_index[s, d] is a cluster of owner s counted within s, or 4 if owner d reads none from s; send_index[d, d] is 4; some owner reads one cluster from every other owner. `near_source`: values at least 4 name an owner s = value - 4 with send_index[s, d] below 4; every cluster that send_index names is used by some near block of its reader.
All inputs are finite; a program needn't handle non-finite values.
Results may differ from the reference program's by a relative error of at most 0.015.
Values may be sent and summed in bfloat16 or wider, within the bound.
A program may use at most 64 MiB of HBM per device.

```python
import math
import jax
import jax.numpy as jnp
from jax import lax

CLS = 256
RANK = 32
RHS = 256
ITERS = 3
CL_DEV = 4
NB_DEV = 30
FB_DEV = 64
NCL = 16
PANELS = 4096
N_BLK = 4
N_COL = 2


def build_plan(key):
    key_full, key_live, key_pick, key_rows, key_fill, key_perm = jax.random.split(key, 6)
    full_owner = jax.random.randint(key_full, (), 0, N_BLK - 1)
    live = jax.random.randint(key_live, (N_BLK, N_BLK), 0, 2)
    target = jnp.arange(N_BLK, dtype=jnp.int32)[:, None]
    anchor = jnp.arange(N_BLK, dtype=jnp.int32)[None, :]
    live = jnp.where(target == full_owner, 1, live)
    live = jnp.where(target == anchor, 0, live)
    picked = jax.random.randint(key_pick, (N_BLK, N_BLK), 0, CL_DEV)
    needed = jnp.where(live == 1, picked, CL_DEV).astype(jnp.int32)
    slots = N_COL * NB_DEV
    position = jnp.arange(slots, dtype=jnp.int32)[None, :]
    fill_src = jax.random.randint(key_fill, (N_BLK, slots), 0, CL_DEV)
    live_ext = jnp.pad(live, ((0, 0), (0, slots - N_BLK)))
    source = jnp.where(live_ext == 1, CL_DEV + position, fill_src)
    diagonal = (position >= N_BLK) & (position < N_BLK + CL_DEV)
    source = jnp.where(diagonal, position - N_BLK, source)
    row_ids = jax.random.randint(key_rows, (N_BLK, slots), 0, CL_DEV)
    row_ids = jnp.where(diagonal, position - N_BLK, row_ids)
    orders = jax.vmap(lambda sub: jax.random.permutation(sub, slots))(jax.random.split(key_perm, N_BLK))
    source = jnp.take_along_axis(source, orders, axis=1)
    row_ids = jnp.take_along_axis(row_ids, orders, axis=1)
    return (needed, row_ids.reshape(-1).astype(jnp.int32), source.reshape(-1).astype(jnp.int32))


def draw_send_index(key, part):
    needed, row_ids, source = build_plan(key)
    return needed.T


def draw_near_rows(key, part):
    needed, row_ids, source = build_plan(key)
    return row_ids


def draw_near_source(key, part):
    needed, row_ids, source = build_plan(key)
    return source


def draw_vector(key, part):
    key = jax.random.fold_in(key, 11)
    key_base, key_scale = jax.random.split(key, 2)
    position = jnp.arange(PANELS, dtype=jnp.float32) / PANELS
    rising = jnp.exp(math.log(3.0) * position)[:, None]
    rising_square = 8.0 / (2.0 * math.log(3.0))
    base = jnp.clip(jax.random.normal(key_base, (PANELS, RHS), jnp.float32), -6.0, 6.0)
    rough = jnp.exp(jax.random.uniform(key_scale, (PANELS, 1), jnp.float32, 0.0, math.log(10.0)))
    spread = math.sqrt(99.0 / (2.0 * math.log(10.0)) * rising_square)
    return jnp.clip(base * rough * rising / spread, -24.0, 24.0).astype(jnp.bfloat16)


def plant(values, own_key, smallest, largest):
    index_at = [jax.random.randint(jax.random.fold_in(own_key, axis), (), 0, length) for axis, length in enumerate(values.shape)]
    longest = values.shape.index(max(values.shape))
    beside = index_at[:longest] + [(index_at[longest] + 1) % values.shape[longest]] + index_at[longest + 1:]
    return values.at[tuple(index_at)].set(smallest).at[tuple(beside)].set(largest)


def block_scale(rng, dims, cuts, smallest, largest):
    factor_of = 1.0
    for axis_at, parts in cuts:
        steps = jax.random.uniform(jax.random.fold_in(jax.random.fold_in(rng, 6), axis_at), (parts,), jnp.float32, smallest / len(cuts), largest / len(cuts))
        factor_of = factor_of * jnp.repeat(jnp.exp(steps), dims[axis_at] // parts).reshape((-1,) + (1,) * (len(dims) - 1 - axis_at))
    return factor_of


def bell_draw(rng, extent, scale, reach, shards=(), held_as=jnp.bfloat16):
    values = jax.random.normal(rng, extent, jnp.float32) * scale
    if len(shards) > 0:
        values = block_scale(rng, extent, shards, -0.22, 0.18) * values
    return jnp.clip(values, min=-reach, max=reach).astype(held_as)


def setup_inputs(seed: int = 0, part: int = 0) -> dict:
    key_list = jax.random.split(jax.random.key(seed), 12)
    own_keys = jax.random.split(jax.random.fold_in(key_list[11], part), 12)
    vector = draw_vector(jax.random.fold_in(jax.random.fold_in(key_list[11], part), 71), part)
    self_term = jnp.clip(jnp.exp(math.log(4.0) - 1.3862944 * jax.random.uniform(own_keys[1], (PANELS,), jnp.float32) ** block_scale(own_keys[1], (PANELS,), ((0, 4),), -0.2, 0.2)), 1.0, 4.0)
    near_blocks = bell_draw(own_keys[2], (N_BLK * N_COL * NB_DEV, CLS, CLS), (CLS * N_COL * NB_DEV // CL_DEV) ** -0.5, 0.09375, ((0, 8),))
    near_rows = draw_near_rows(jax.random.fold_in(jax.random.fold_in(key_list[11], part), 71), part)
    near_source = draw_near_source(jax.random.fold_in(jax.random.fold_in(key_list[11], part), 71), part)
    send_index = draw_send_index(jax.random.fold_in(jax.random.fold_in(key_list[11], part), 71), part)
    source_basis = bell_draw(own_keys[6], (NCL, RANK, CLS), CLS ** -0.5, 0.375, ((0, 4),))
    target_basis = bell_draw(own_keys[7], (NCL, RANK, CLS), RANK ** -0.5, 1.0, ((0, 4),))
    couplings = bell_draw(own_keys[8], (N_BLK * N_COL * FB_DEV, RANK, RANK), (RANK * N_COL * FB_DEV // CL_DEV) ** -0.5, 0.1875, ((0, 8),))
    far_rows = plant(jax.random.randint(own_keys[9], (N_BLK * N_COL * FB_DEV,), 0, CL_DEV), jax.random.fold_in(own_keys[9], 1), 0, CL_DEV - 1).astype(jnp.int32)
    far_cols = plant(jax.random.randint(own_keys[10], (N_BLK * N_COL * FB_DEV,), 0, NCL), jax.random.fold_in(own_keys[10], 1), 0, NCL - 1).astype(jnp.int32)
    return {"vector": vector, "self_term": self_term, "near_blocks": near_blocks, "near_rows": near_rows, "near_source": near_source, "send_index": send_index, "source_basis": source_basis, "target_basis": target_basis, "couplings": couplings, "far_rows": far_rows, "far_cols": far_cols}


def apply_operator(current, self_term, blocks, near_rows, near_source, send_index, source_basis, target_basis, couplings, far_rows, far_cols):
    segs = current.reshape(NCL, CLS, RHS)
    padded = jnp.concatenate([segs, jnp.zeros((1, CLS, RHS), jnp.bfloat16)], axis=0)
    per_near = N_COL * NB_DEV
    per_far = N_COL * FB_DEV

    def owner_near(items):
        owner, tiles, rows_ids, source_ids, reads = items
        own = lax.dynamic_slice_in_dim(segs, (owner * CL_DEV).astype(jnp.int32), CL_DEV, 0)
        remote_ids = jnp.where(reads < CL_DEV, jnp.arange(N_BLK, dtype=jnp.int32) * CL_DEV + reads, NCL).astype(jnp.int32)
        sources = jnp.concatenate([own, padded[remote_ids]], axis=0)
        picked = sources[source_ids].astype(jnp.float32)
        products = jnp.einsum('bij,bjw->biw', tiles.astype(jnp.float32), picked, precision=lax.Precision.HIGHEST)
        onehot = (rows_ids[None, :] == jnp.arange(CL_DEV, dtype=jnp.int32)[:, None]).astype(jnp.float32)
        return jnp.einsum('rb,biw->riw', onehot, products, precision=lax.Precision.HIGHEST)
    near = lax.map(owner_near, (jnp.arange(N_BLK, dtype=jnp.int32), blocks.reshape(N_BLK, per_near, CLS, CLS), near_rows.reshape(N_BLK, per_near), near_source.reshape(N_BLK, per_near), send_index.T))
    coef = jnp.einsum('krc,kcw->krw', source_basis.astype(jnp.float32), segs.astype(jnp.float32), precision=lax.Precision.HIGHEST).astype(jnp.bfloat16)

    def owner_far(items):
        mats, rows_ids, cols_ids = items
        chosen = coef[cols_ids].astype(jnp.float32)
        mixed = jnp.einsum('fab,fbw->faw', mats.astype(jnp.float32), chosen, precision=lax.Precision.HIGHEST)
        onehot = (rows_ids[None, :] == jnp.arange(CL_DEV, dtype=jnp.int32)[:, None]).astype(jnp.float32)
        return jnp.einsum('rf,faw->raw', onehot, mixed, precision=lax.Precision.HIGHEST)
    zeta = lax.map(owner_far, (couplings.reshape(N_BLK, per_far, RANK, RANK), far_rows.reshape(N_BLK, per_far), far_cols.reshape(N_BLK, per_far)))
    zeta = zeta.reshape(NCL, RANK, RHS)
    far = jnp.einsum('kac,kaw->kcw', target_basis.astype(jnp.float32), zeta, precision=lax.Precision.HIGHEST)
    total = near.reshape(PANELS, RHS) + far.reshape(PANELS, RHS)
    return total + self_term[:, None] * current.astype(jnp.float32)

def reference(vector, self_term, near_blocks, near_rows, near_source, send_index, source_basis, target_basis, couplings, far_rows, far_cols):
    basis = [vector]
    entries = []
    for step in range(ITERS):
        work = apply_operator(basis[-1], self_term, near_blocks, near_rows, near_source, send_index, source_basis, target_basis, couplings, far_rows, far_cols)
        coefs = [lax.optimization_barrier(jnp.sum(member.astype(jnp.float32) * work, axis=0)) / PANELS for member in basis]
        for member, value in zip(basis, coefs):
            work = work - value[None, :] * member.astype(jnp.float32)
        beta = jnp.sqrt(lax.optimization_barrier(jnp.sum(work * work, axis=0)) / PANELS + 1e-06)
        fresh = (work / beta[None, :]).astype(jnp.bfloat16)
        entries = entries + coefs + [beta]
        basis.append(fresh)
    return (basis[-1], jnp.stack(entries))
```

```python
import functools

import jax
import jax.numpy as jnp
from jax import lax
from jax.experimental import pallas as pl
from jax.experimental.pallas import tpu as pltpu
from jax.sharding import PartitionSpec as P

ITERS = 3
MESH = pl.DeviceIdType.MESH


def dot(a, b):
    return jnp.dot(a, b, preferred_element_type=jnp.float32)


def pack_kernel(rows_ref, cols_ref, frows_ref, fcols_ref, near_ref, coup_ref, target_ref,
                dense_ref, far_ref, lift_ref, cells):
    cls = near_ref.shape[1]
    rank = coup_ref.shape[1]
    dense_ref[...] = jnp.zeros_like(dense_ref)
    cells[...] = jnp.zeros_like(cells)

    @pl.loop(0, near_ref.shape[0])
    def _(b):
        where = (rows_ref[b], slice(None), pl.ds(pl.multiple_of(cols_ref[b] * cls, cls), cls))
        dense_ref[where] += near_ref[b]

    @pl.loop(0, coup_ref.shape[0])
    def _(f):
        at = pl.ds(pl.multiple_of(frows_ref[f] * rank, rank), rank)
        cells[fcols_ref[f], at, :] += coup_ref[f].astype(jnp.float32)

    for c in range(cells.shape[0]):
        far_ref[:, c * rank:(c + 1) * rank] = cells[c].astype(jnp.bfloat16)
    for r in range(target_ref.shape[0]):
        lift_ref[r] = target_ref[r].astype(jnp.float32).T.astype(jnp.bfloat16)


def solve_kernel(n, ncol, send_ref, vector_ref, self_ref, dense_ref, far_ref, source_ref, lift_ref,
                 last_ref, hess_ref,
                 basis, work, seg_out, seg_in, coef, parts, dots,
                 seg_s, seg_r, coef_s, coef_r, part_s, part_r, dot_s, dot_r):
    me = lax.axis_index("blk")
    mycol = lax.axis_index("col")
    owned, cls, width = vector_ref.shape
    rank = source_ref.shape[1]
    panels = n * owned * cls
    barrier = pltpu.get_barrier_semaphore()
    for j in range(1, n):
        pl.semaphore_signal(barrier, inc=1, device_id={"blk": lax.rem(me + j, n)}, device_id_type=MESH)
    for j in range(1, ncol):
        pl.semaphore_signal(barrier, inc=1, device_id={"col": lax.rem(mycol + j, ncol)}, device_id_type=MESH)
    pl.semaphore_wait(barrier, n - 1 + ncol - 1)

    pending = []
    gram = {}
    line = 0

    def member(i):
        return vector_ref if i == 0 else basis.at[i - 1]

    def send(src, dst, ssem, rsem, axis, peer):
        copy = pltpu.make_async_remote_copy(src_ref=src, dst_ref=dst, send_sem=ssem, recv_sem=rsem,
                                            device_id={axis: peer}, device_id_type=MESH)
        copy.start()
        pending.append(copy)

    def arrived(dst, rsem):
        pltpu.make_async_copy(dst, dst, rsem).wait()

    for step in range(ITERS):
        current = member(step)
        for j in range(1, n):
            peer = lax.rem(me + j, n)
            pick = jnp.minimum(send_ref[0, peer], owned - 1)
            seg_out[step, j - 1] = current[pick]
            send(seg_out.at[step, j - 1], seg_in.at[step, n - j - 1],
                 seg_s.at[step, j - 1], seg_r.at[step, n - j - 1], "blk", peer)
        for c in range(owned):
            coef[step, me, c * rank:(c + 1) * rank, :] = dot(source_ref[c], current[c]).astype(jnp.bfloat16)
        for j in range(1, n):
            send(coef.at[step, me], coef.at[step, me], coef_s.at[step, j - 1], coef_r.at[step, n - j - 1],
                 "blk", lax.rem(me + j, n))
        mine = current[...].reshape(owned * cls, width)
        for r in range(owned):
            work[r] = dot(dense_ref[r, :, :owned * cls], mine)
        for j in range(1, n):
            arrived(coef.at[step, lax.rem(me + j, n)], coef_r.at[step, j - 1])
        zeta = dot(far_ref[...], coef[step].reshape(n * owned * rank, width)).astype(jnp.bfloat16)
        for j in range(1, n):
            arrived(seg_in.at[step, j - 1], seg_r.at[step, j - 1])
        theirs = seg_in[step].reshape((n - 1) * cls, width)
        for r in range(owned):
            total = work[r] + dot(dense_ref[r, :, owned * cls:], theirs)
            total = total + dot(lift_ref[r], zeta[r * rank:(r + 1) * rank])
            parts[step, r, mycol] = total.astype(jnp.bfloat16)
            for j in range(1, ncol):
                send(parts.at[step, r, mycol], parts.at[step, r, mycol],
                     part_s.at[step, r, j - 1], part_r.at[step, r, ncol - j - 1],
                     "col", lax.rem(mycol + j, ncol))
        count = step + 1
        sums = [0.0] * (2 * count + 1)
        for r in range(owned):
            newest = current[r].astype(jnp.float32)
            for i in range(count):
                other = newest if i == step else member(i)[r].astype(jnp.float32)
                sums[count + 1 + i] += jnp.sum(newest * other, axis=0, keepdims=True)
        for r in range(owned):
            for j in range(1, ncol):
                arrived(parts.at[step, r, lax.rem(mycol + j, ncol)], part_r.at[step, r, j - 1])
            total = self_ref[r] * current[r].astype(jnp.float32)
            for k in range(ncol):
                total = total + parts[step, r, k].astype(jnp.float32)
            work[r] = total
            for i in range(count):
                sums[i] += jnp.sum(total * member(i)[r].astype(jnp.float32), axis=0, keepdims=True)
            sums[count] += jnp.sum(total * total, axis=0, keepdims=True)
        pad = [jnp.zeros((1, width), jnp.float32)] * (8 - len(sums))
        dots[step, me] = jnp.concatenate(sums + pad, axis=0)
        for j in range(1, n):
            send(dots.at[step, me], dots.at[step, me], dot_s.at[step, j - 1], dot_r.at[step, n - j - 1],
                 "blk", lax.rem(me + j, n))
        for j in range(1, n):
            arrived(dots.at[step, lax.rem(me + j, n)], dot_r.at[step, j - 1])
        total = dots[step, 0]
        for k in range(1, n):
            total = total + dots[step, k]
        total = total / panels
        coefs = [total[i:i + 1] for i in range(count)]
        for i in range(count):
            gram[i, step] = gram[step, i] = total[count + 1 + i:count + 2 + i]
        square = total[count:count + 1]
        for i in range(count):
            inner = -2.0 * coefs[i]
            for k in range(count):
                inner = inner + coefs[k] * gram[i, k]
            square = square + coefs[i] * inner
        beta = jnp.sqrt(jnp.maximum(square, 0.0) + 1e-06)
        scale = 1.0 / beta
        for value in coefs + [beta]:
            hess_ref[line:line + 1, :] = value
            line += 1
        if step < ITERS - 1:
            for r in range(owned):
                fresh = work[r]
                for i in range(count):
                    fresh = fresh - coefs[i] * member(i)[r].astype(jnp.float32)
                basis[step, r] = (fresh * scale).astype(jnp.bfloat16)
        else:
            share = owned * cls // ncol
            at = pl.multiple_of(mycol * share, share)
            fresh = work.reshape(owned * cls, width)[pl.ds(at, share)]
            for i in range(count):
                fresh = fresh - coefs[i] * member(i).reshape(owned * cls, width)[pl.ds(at, share)].astype(jnp.float32)
            last_ref[...] = (fresh * scale).astype(jnp.bfloat16)
    for copy in pending:
        copy.wait_send()


def on_device(vector, self_term, near_blocks, near_rows, near_source, send_index, source_basis,
              target_basis, couplings, far_rows, far_cols):
    owned, rank, cls = source_basis.shape
    width = vector.shape[1]
    n = lax.axis_size("blk")
    ncol = lax.axis_size("col")
    me = lax.axis_index("blk")
    clusters = n * owned
    sources = owned + n - 1
    bf16, f32 = jnp.bfloat16, jnp.float32
    place = jnp.where(near_source < owned, near_source,
                      owned - 1 + lax.rem(near_source - owned - me + n, n))
    vmem, smem = pl.BlockSpec(memory_space=pltpu.VMEM), pl.BlockSpec(memory_space=pltpu.SMEM)
    dense, far, lift = pl.pallas_call(
        pack_kernel,
        out_shape=(
            jax.ShapeDtypeStruct((owned, cls, sources * cls), bf16),
            jax.ShapeDtypeStruct((owned * rank, clusters * rank), bf16),
            jax.ShapeDtypeStruct((owned, cls, rank), bf16),
        ),
        in_specs=[smem] * 4 + [vmem] * 3,
        out_specs=(vmem,) * 3,
        scratch_shapes=[pltpu.VMEM((clusters, owned * rank, rank), f32)],
        compiler_params=pltpu.CompilerParams(vmem_limit_bytes=50 << 20),
        name="pack",
    )(near_rows, place, far_rows, far_cols, near_blocks, couplings, target_basis)
    dma = pltpu.SemaphoreType.DMA
    wide_self = jnp.broadcast_to(self_term.reshape(owned, cls, 1), (owned, cls, width))
    return pl.pallas_call(
        functools.partial(solve_kernel, n, ncol),
        out_shape=(
            jax.ShapeDtypeStruct((owned * cls // ncol, width), bf16),
            jax.ShapeDtypeStruct((ITERS * (ITERS + 3) // 2, width), f32),
        ),
        in_specs=[smem] + [vmem] * 6,
        out_specs=(vmem, vmem),
        scratch_shapes=[
            pltpu.VMEM((ITERS - 1, owned, cls, width), bf16),
            pltpu.VMEM((owned, cls, width), f32),
            pltpu.VMEM((ITERS, n - 1, cls, width), bf16),
            pltpu.VMEM((ITERS, n - 1, cls, width), bf16),
            pltpu.VMEM((ITERS, n, owned * rank, width), bf16),
            pltpu.VMEM((ITERS, owned, ncol, cls, width), bf16),
            pltpu.VMEM((ITERS, n, 8, width), f32),
            dma((ITERS, n - 1)), dma((ITERS, n - 1)),
            dma((ITERS, n - 1)), dma((ITERS, n - 1)),
            dma((ITERS, owned, ncol - 1)), dma((ITERS, owned, ncol - 1)),
            dma((ITERS, n - 1)), dma((ITERS, n - 1)),
        ],
        compiler_params=pltpu.CompilerParams(collective_id=0, has_side_effects=True, vmem_limit_bytes=50 << 20),
        name="solve",
    )(send_index, vector.reshape(owned, cls, width), wide_self, dense, far, source_basis, lift)


def solution(mesh):
    placed = (
        P(("grp", "blk"), "rhs"),
        P(("grp", "blk")),
        P(("grp", "blk", "col"), None, None),
        P(("grp", "blk", "col")),
        P(("grp", "blk", "col")),
        P(("grp", "blk"), None),
        P(("grp", "blk"), None, None),
        P(("grp", "blk"), None, None),
        P(("grp", "blk", "col"), None, None),
        P(("grp", "blk", "col")),
        P(("grp", "blk", "col")),
    )
    return jax.shard_map(
        on_device,
        mesh=mesh,
        in_specs=placed,
        out_specs=(P(("grp", "blk", "col"), "rhs"), P("grp", "rhs")),
        check_vma=False,
    )
```

```python
import functools

import jax
import jax.numpy as jnp
from jax import lax
from jax.experimental import pallas as pl
from jax.experimental.pallas import tpu as pltpu
from jax.sharding import PartitionSpec as P

ITERS = 3
MESH = pl.DeviceIdType.MESH


def dot(a, b):
    return jnp.dot(a, b, preferred_element_type=jnp.float32)


def pack(n, rows, cols, near_in, coup_ref, frows_ref, target_ref, cells, keys, turned, dense, far, lift, near_sem):
    me = lax.axis_index("blk")
    count, cls, _ = near_in.shape
    owned = target_ref.shape[0]
    rank = turned.shape[0]
    sources = owned + n - 1
    fetch = pltpu.make_async_copy(near_in, cells.at[pl.ds(0, count)], near_sem)
    fetch.start()
    cells[count] = jnp.zeros((cls, cls), jnp.bfloat16)
    for b in range(count):
        source = cols[b]
        place = jnp.where(source < owned, source, owned - 1 + lax.rem(source - owned - me + n, n))
        keys[b] = rows[b] * sources + place

    for k in range(rank):
        turned[k] = coup_ref[k].astype(jnp.float32).T
    per = 128 // rank
    lane = lax.broadcasted_iota(jnp.int32, (rank, 128), 1)
    for g in range(frows_ref.shape[0] // per):
        wide = jnp.concatenate([turned[:, g * per + i, :] for i in range(per)], axis=1)
        row = jnp.full((rank, 128), frows_ref[g * per], jnp.int32)
        for i in range(1, per):
            row = jnp.where(lane >= i * rank, frows_ref[g * per + i], row)
        for r in range(owned):
            far[r * rank:(r + 1) * rank, g * 128:(g + 1) * 128] = jnp.where(row == r, wide, 0.0).astype(jnp.bfloat16)
    for r in range(owned):
        lift[r] = target_ref[r].astype(jnp.float32).T.astype(jnp.bfloat16)

    def latest(key, limit):
        found = jnp.int32(count)
        for b in range(count):
            hit = keys[b] == key
            if limit is not None:
                hit = jnp.logical_and(hit, b < limit)
            found = jnp.where(hit, b, found)
        return found

    fetch.wait()

    @pl.loop(0, count)
    def _(b):
        cells[b] = cells[b] + cells[latest(keys[b], b)]

    @pl.loop(0, owned)
    def _(r):
        for c in range(sources):
            dense[r, :, c * cls:(c + 1) * cls] = cells[latest(r * sources + c, None)]


def solve_kernel(n, ncol, rows, cols, send_ref, frows_ref, fcols_ref, near_in, vector_ref, self_ref,
                 source_ref, target_ref, coup_ref,
                 last_ref, hess_ref,
                 cells, keys, turned, dense, far, lift,
                 basis, work, outgoing, incoming, seg, raw, coef, chosen, parts, dots,
                 near_sem, out_s, in_r, fwd_s, fwd_r, part_s, part_r, dot_s, dot_r):
    me = lax.axis_index("blk")
    mycol = lax.axis_index("col")
    owned, cls, width = vector_ref.shape
    rank = source_ref.shape[1]
    panels = n * owned * cls
    block = owned * rank
    share, cshare = cls // ncol, block // ncol
    everyone = [(j, c) for j in range(n) for c in range(ncol) if j or c]
    barrier = pltpu.get_barrier_semaphore()

    def at(j, c):
        return {"blk": lax.rem(me + j, n), "col": lax.rem(mycol + c, ncol)}

    for j, c in everyone:
        pl.semaphore_signal(barrier, inc=1, device_id=at(j, c), device_id_type=MESH)
    pl.semaphore_wait(barrier, len(everyone))

    pending = []
    gram = {}
    line = 0

    def member(i):
        return vector_ref if i == 0 else basis.at[i - 1]

    def send(src, dst, ssem, rsem, j, c):
        copy = pltpu.make_async_remote_copy(src_ref=src, dst_ref=dst, send_sem=ssem, recv_sem=rsem,
                                            device_id=at(j, c), device_id_type=MESH)
        copy.start()
        pending.append(copy)

    def arrived(dst, rsem):
        pltpu.make_async_copy(dst, dst, rsem).wait()

    def owner_rows(j):
        return pl.multiple_of(lax.rem(me + j, n) * block, block)

    def share_out(step, field):
        for c in range(owned):
            raw[pl.ds(owner_rows(0) + c * rank, rank), :] = dot(
                source_ref[c], field[c].astype(jnp.bfloat16)).astype(jnp.bfloat16)
        mine = raw[pl.ds(pl.multiple_of(owner_rows(0) + mycol * cshare, cshare), cshare), :]
        for j in range(1, n):
            pick = jnp.minimum(send_ref[0, lax.rem(me + j, n)], owned - 1)
            outgoing[step, j - 1, :share] = field[pick, pl.ds(pl.multiple_of(mycol * share, share), share), :].astype(jnp.bfloat16)
            outgoing[step, j - 1, share:] = mine
            send(outgoing.at[step, j - 1], incoming.at[step, n - j - 1, mycol],
                 out_s.at[step, j - 1], in_r.at[step, n - j - 1], j, 0)

    def pass_on(step):
        for j in range(1, n):
            here = incoming.at[step, j - 1, mycol]
            arrived(here, in_r.at[step, j - 1])
            for c in range(1, ncol):
                send(here, here, fwd_s.at[step, j - 1, c - 1], fwd_r.at[step, j - 1, ncol - c - 1], 0, c)

    def collect(step):
        for j in range(1, n):
            for c in range(1, ncol):
                arrived(incoming.at[step, j - 1, lax.rem(mycol + c, ncol)], fwd_r.at[step, j - 1, c - 1])
            for k in range(ncol):
                seg[step, j - 1, k * share:(k + 1) * share] = incoming[step, j - 1, k, :share]
                raw[pl.ds(pl.multiple_of(owner_rows(j) + k * cshare, cshare), cshare), :] = incoming[step, j - 1, k, share:]

    share_out(0, vector_ref)
    pack(n, rows, cols, near_in, coup_ref, frows_ref, target_ref, cells, keys, turned, dense, far, lift, near_sem)
    coefs, scale = [], None
    for step in range(ITERS):
        current = member(step)
        final = step == ITERS - 1
        pass_on(step)
        mine = current[...].reshape(owned * cls, width)
        for r in range(owned):
            work[r] = dot(dense[r, :, :owned * cls], mine)
        collect(step)
        if step == 0:
            coef[0] = raw[...].reshape(n * owned, rank, width)
        else:
            fresh = raw[...].reshape(n * owned, rank, width).astype(jnp.float32)
            for i in range(step):
                fresh = fresh - coefs[i] * coef[i].astype(jnp.float32)
            coef[step] = (fresh * scale).astype(jnp.bfloat16)
            for j in range(n - 1):
                fresh = seg[step, j].astype(jnp.float32)
                for i in range(step):
                    fresh = fresh - coefs[i] * seg[i, j].astype(jnp.float32)
                seg[step, j] = (fresh * scale).astype(jnp.bfloat16)
        for f in range(fcols_ref.shape[0]):
            chosen[f * rank:(f + 1) * rank] = coef[step, fcols_ref[f]]
        zeta = dot(far[...], chosen[...]).astype(jnp.bfloat16)
        chosen[:block] = zeta
        theirs = seg[step].reshape((n - 1) * cls, width)

        def total_of(r):
            total = work[r] + dot(dense[r, :, owned * cls:], theirs)
            zeta_r = chosen[pl.ds(pl.multiple_of(r * rank, rank), rank), :]
            return (total + dot(lift[r], zeta_r)).astype(jnp.bfloat16)

        if final:
            each = owned // ncol
            first = [(c, i, lax.rem(mycol + c, ncol) * each + i) for c in range(1, ncol) for i in range(each)]
            for c, i, r in first:
                parts[step, r, mycol] = total_of(r)
                send(parts.at[step, r, mycol], parts.at[step, r, mycol],
                     part_s.at[step, i, c - 1], part_r.at[step, i, ncol - c - 1], 0, c)
            held = [mycol * each + i for i in range(each)]
            for r in held:
                parts[step, r, mycol] = total_of(r)
        else:
            held = list(range(owned))
            for r in held:
                parts[step, r, mycol] = total_of(r)
                for c in range(1, ncol):
                    send(parts.at[step, r, mycol], parts.at[step, r, mycol],
                         part_s.at[step, r, c - 1], part_r.at[step, r, ncol - c - 1], 0, c)
        count = step + 1
        sums = [0.0] * (2 * count + 1)
        for r in held:
            newest = current[r].astype(jnp.float32)
            for i in range(count):
                other = newest if i == step else member(i)[r].astype(jnp.float32)
                sums[count + 1 + i] += jnp.sum(newest * other, axis=0, keepdims=True)
        for i, r in enumerate(held):
            for c in range(1, ncol):
                arrived(parts.at[step, r, lax.rem(mycol + c, ncol)], part_r.at[step, i, c - 1])
            total = self_ref[r] * current[r].astype(jnp.float32)
            for k in range(ncol):
                total = total + parts[step, r, k].astype(jnp.float32)
            work[r] = total
            for i in range(count):
                sums[i] += jnp.sum(total * member(i)[r].astype(jnp.float32), axis=0, keepdims=True)
            sums[count] += jnp.sum(total * total, axis=0, keepdims=True)
        pad = [jnp.zeros((1, width), jnp.float32)] * (8 - len(sums))
        slot = me * ncol + mycol if final else me
        dots[step, slot] = jnp.concatenate(sums + pad, axis=0)
        peers = everyone if final else [(j, 0) for j in range(1, n)]
        for j, c in peers:
            send(dots.at[step, slot], dots.at[step, slot], dot_s.at[step, j, c],
                 dot_r.at[step, (n - j) % n, (ncol - c) % ncol], j, c)
        if not final:
            share_out(step + 1, work)
        for j, c in peers:
            theirs_at = lax.rem(me + j, n)
            if final:
                theirs_at = theirs_at * ncol + lax.rem(mycol + c, ncol)
            arrived(dots.at[step, theirs_at], dot_r.at[step, j, c])
        total = dots[step, 0]
        for k in range(1, n * ncol if final else n):
            total = total + dots[step, k]
        total = total / panels
        coefs = [total[i:i + 1] for i in range(count)]
        for i in range(count):
            gram[i, step] = gram[step, i] = total[count + 1 + i:count + 2 + i]
        square = total[count:count + 1]
        for i in range(count):
            inner = -2.0 * coefs[i]
            for k in range(count):
                inner = inner + coefs[k] * gram[i, k]
            square = square + coefs[i] * inner
        beta = jnp.sqrt(jnp.maximum(square, 0.0) + 1e-06)
        scale = 1.0 / beta
        for value in coefs + [beta]:
            hess_ref[line:line + 1, :] = value
            line += 1
        for i, r in enumerate(held):
            fresh = work[r]
            for k in range(count):
                fresh = fresh - coefs[k] * member(k)[r].astype(jnp.float32)
            fresh = (fresh * scale).astype(jnp.bfloat16)
            if final:
                last_ref[i * cls:(i + 1) * cls] = fresh
            else:
                basis[step, r] = fresh
    for copy in pending:
        copy.wait_send()


def on_device(vector, self_term, near_blocks, near_rows, near_source, send_index, source_basis,
              target_basis, couplings, far_rows, far_cols):
    owned, rank, cls = source_basis.shape
    width = vector.shape[1]
    n = lax.axis_size("blk")
    ncol = lax.axis_size("col")
    count, links = near_blocks.shape[0], couplings.shape[0]
    block = owned * rank
    piece = (cls + block) // ncol
    bf16, f32 = jnp.bfloat16, jnp.float32
    vmem, smem = pl.BlockSpec(memory_space=pltpu.VMEM), pl.BlockSpec(memory_space=pltpu.SMEM)
    hbm = pl.BlockSpec(memory_space=pl.ANY)
    dma = pltpu.SemaphoreType.DMA
    wide_self = jnp.broadcast_to(self_term.reshape(owned, cls, 1), (owned, cls, width))
    return pl.pallas_call(
        functools.partial(solve_kernel, n, ncol),
        out_shape=(
            jax.ShapeDtypeStruct((owned * cls // ncol, width), bf16),
            jax.ShapeDtypeStruct((ITERS * (ITERS + 3) // 2, width), f32),
        ),
        in_specs=[smem] * 5 + [hbm] + [vmem] * 5,
        out_specs=(vmem, vmem),
        scratch_shapes=[
            pltpu.VMEM((count + 1, cls, cls), bf16),
            pltpu.SMEM((count,), jnp.int32),
            pltpu.VMEM((rank, links, rank), f32),
            pltpu.VMEM((owned, cls, (owned + n - 1) * cls), bf16),
            pltpu.VMEM((block, links * rank), bf16),
            pltpu.VMEM((owned, cls, rank), bf16),
            pltpu.VMEM((ITERS - 1, owned, cls, width), bf16),
            pltpu.VMEM((owned, cls, width), f32),
            pltpu.VMEM((ITERS, n - 1, piece, width), bf16),
            pltpu.VMEM((ITERS, n - 1, ncol, piece, width), bf16),
            pltpu.VMEM((ITERS, n - 1, cls, width), bf16),
            pltpu.VMEM((n * block, width), bf16),
            pltpu.VMEM((ITERS, n * owned, rank, width), bf16),
            pltpu.VMEM((max(links * rank, block), width), bf16),
            pltpu.VMEM((ITERS, owned, ncol, cls, width), bf16),
            pltpu.VMEM((ITERS, n * ncol, 8, width), f32),
            dma,
            dma((ITERS, n - 1)), dma((ITERS, n - 1)),
            dma((ITERS, n - 1, ncol - 1)), dma((ITERS, n - 1, ncol - 1)),
            dma((ITERS, owned, ncol - 1)), dma((ITERS, owned, ncol - 1)),
            dma((ITERS, n, ncol)), dma((ITERS, n, ncol)),
        ],
        compiler_params=pltpu.CompilerParams(collective_id=0, has_side_effects=True, vmem_limit_bytes=59 << 20),
        name="solve",
    )(near_rows, near_source, send_index, far_rows, far_cols, near_blocks,
      vector.reshape(owned, cls, width), wide_self, source_basis, target_basis,
      couplings.transpose(1, 2, 0))


def solution(mesh):
    placed = (
        P(("grp", "blk"), "rhs"),
        P(("grp", "blk")),
        P(("grp", "blk", "col"), None, None),
        P(("grp", "blk", "col")),
        P(("grp", "blk", "col")),
        P(("grp", "blk"), None),
        P(("grp", "blk"), None, None),
        P(("grp", "blk"), None, None),
        P(("grp", "blk", "col"), None, None),
        P(("grp", "blk", "col")),
        P(("grp", "blk", "col")),
    )
    return jax.shard_map(
        on_device,
        mesh=mesh,
        in_specs=placed,
        out_specs=(P(("grp", "blk", "col"), "rhs"), P("grp", "rhs")),
        check_vma=False,
    )
```

```python
import functools

import jax
import jax.numpy as jnp
from jax import lax
from jax.experimental import pallas as pl
from jax.experimental.pallas import tpu as pltpu
from jax.sharding import PartitionSpec as P

ITERS = 3
MESH = pl.DeviceIdType.MESH


def dot(a, b):
    return jnp.dot(a, b, preferred_element_type=jnp.float32)


def pack(n, rows, cols, near_in, coup_ref, frows_ref, target_ref, self_ref, cells, keys, turned, dense, far, lift,
         diagonal, near_sem, between):
    me = lax.axis_index("blk")
    count, cls, _ = near_in.shape
    owned = target_ref.shape[0]
    rank = turned.shape[0]
    sources = owned + n - 1
    fetch = pltpu.make_async_copy(near_in, cells.at[pl.ds(0, count)], near_sem)
    fetch.start()
    cells[count] = jnp.zeros((cls, cls), jnp.bfloat16)
    for b in range(count):
        source = cols[b]
        place = jnp.where(source < owned, source, owned - 1 + lax.rem(source - owned - me + n, n))
        keys[b] = rows[b] * sources + place

    for k in range(rank):
        turned[k] = coup_ref[k].astype(jnp.float32).T
    per = 128 // rank
    lane = lax.broadcasted_iota(jnp.int32, (rank, 128), 1)
    for g in range(frows_ref.shape[0] // per):
        wide = jnp.concatenate([turned[:, g * per + i, :] for i in range(per)], axis=1)
        row = jnp.full((rank, 128), frows_ref[g * per], jnp.int32)
        for i in range(1, per):
            row = jnp.where(lane >= i * rank, frows_ref[g * per + i], row)
        for r in range(owned):
            far[r * rank:(r + 1) * rank, g * 128:(g + 1) * 128] = jnp.where(row == r, wide, 0.0).astype(jnp.bfloat16)
    for r in range(owned):
        lift[r] = target_ref[r].astype(jnp.float32).T.astype(jnp.bfloat16)

    def latest(key, limit):
        found = jnp.int32(count)
        for b in range(count):
            hit = keys[b] == key
            if limit is not None:
                hit = jnp.logical_and(hit, b < limit)
            found = jnp.where(hit, b, found)
        return found

    for i in range(self_ref.shape[0]):
        column = jnp.broadcast_to(self_ref[i:i + 1], (diagonal.shape[1], 128)).T
        diagonal[i * 128:(i + 1) * 128] = column
    between()
    fetch.wait()

    @pl.loop(0, count)
    def _(b):
        cells[b] = cells[b] + cells[latest(keys[b], b)]

    @pl.loop(0, owned)
    def _(r):
        for c in range(sources):
            dense[r, :, c * cls:(c + 1) * cls] = cells[latest(r * sources + c, None)]


def solve_kernel(n, ncol, rows, cols, send_ref, frows_ref, fcols_ref, near_in, vector_ref, self_ref,
                 source_ref, target_ref, coup_ref,
                 last_ref, hess_ref,
                 cells, keys, turned, dense, far, lift, diagonal,
                 basis, work, outgoing, incoming, seg, raw, coef, chosen, parts, dots,
                 near_sem, out_s, in_r, fwd_s, fwd_r, coef_s, coef_r, part_s, part_r, dot_s, dot_r):
    me = lax.axis_index("blk")
    mycol = lax.axis_index("col")
    owned, cls, width = vector_ref.shape
    rank = source_ref.shape[1]
    panels = n * owned * cls
    block = owned * rank
    share = cls // ncol
    everyone = [(j, c) for j in range(n) for c in range(ncol) if j or c]
    barrier = pltpu.get_barrier_semaphore()

    def at(j, c):
        return {"blk": lax.rem(me + j, n), "col": lax.rem(mycol + c, ncol)}

    for j, c in everyone:
        pl.semaphore_signal(barrier, inc=1, device_id=at(j, c), device_id_type=MESH)
    pl.semaphore_wait(barrier, len(everyone))

    pending = []
    gram = {}
    line = 0

    def member(i):
        return vector_ref if i == 0 else basis.at[i - 1]

    def send(src, dst, ssem, rsem, j, c):
        copy = pltpu.make_async_remote_copy(src_ref=src, dst_ref=dst, send_sem=ssem, recv_sem=rsem,
                                            device_id=at(j, c), device_id_type=MESH)
        copy.start()
        pending.append(copy)

    def arrived(dst, rsem):
        pltpu.make_async_copy(dst, dst, rsem).wait()

    def share_coef(step, c, field):
        mine = raw.at[step, me * owned + c]
        mine[...] = dot(source_ref[c], field.astype(jnp.bfloat16)).astype(jnp.bfloat16)
        for j in range(1, n):
            send(mine, mine, coef_s.at[step, c, j - 1], coef_r.at[step, c, n - j - 1], j, 0)

    def share_segments(step, field):
        for j in range(1, n):
            pick = jnp.minimum(send_ref[0, lax.rem(me + j, n)], owned - 1)
            part = field[pick, pl.ds(pl.multiple_of(mycol * share, share), share), :]
            outgoing[step, j - 1] = part.astype(jnp.bfloat16)
            send(outgoing.at[step, j - 1], incoming.at[step, n - j - 1, mycol],
                 out_s.at[step, j - 1], in_r.at[step, n - j - 1], j, 0)

    def pass_on(step):
        for j in range(1, n):
            here = incoming.at[step, j - 1, mycol]
            arrived(here, in_r.at[step, j - 1])
            for c in range(1, ncol):
                send(here, here, fwd_s.at[step, j - 1, c - 1], fwd_r.at[step, j - 1, ncol - c - 1], 0, c)

    def collect(step):
        for j in range(1, n):
            for c in range(1, ncol):
                arrived(incoming.at[step, j - 1, lax.rem(mycol + c, ncol)], fwd_r.at[step, j - 1, c - 1])

    def collect_coefs(step):
        for c in range(owned):
            for j in range(1, n):
                arrived(raw.at[step, lax.rem(me + j, n) * owned + c], coef_r.at[step, c, j - 1])

    share_segments(0, vector_ref)
    for c in range(owned):
        share_coef(0, c, vector_ref[c])
    pack(n, rows, cols, near_in, coup_ref, frows_ref, target_ref, self_ref, cells, keys, turned, dense, far, lift,
         diagonal, near_sem, lambda: pass_on(0))
    coefs, scale = [], None
    for step in range(ITERS):
        current = member(step)
        final = step == ITERS - 1
        mine = current[...].reshape(owned * cls, width)
        for r in range(owned):
            work[r] = dot(dense[r, :, :owned * cls], mine)
        collect_coefs(step)
        fresh = raw[step]
        if step:
            fresh = fresh.astype(jnp.float32)
            for i in range(step):
                fresh = fresh - coefs[i] * coef[i].astype(jnp.float32)
            fresh = (fresh * scale).astype(jnp.bfloat16)
        coef[step] = fresh
        for f in range(fcols_ref.shape[0]):
            chosen[f * rank:(f + 1) * rank] = coef[step, fcols_ref[f]]
        zeta = dot(far[...], chosen[...]).astype(jnp.bfloat16)
        for r in range(owned):
            work[r] += dot(lift[r], zeta[r * rank:(r + 1) * rank])
        collect(step)
        for j in range(n - 1):
            fresh = incoming[step, j].reshape(cls, width)
            if step:
                fresh = fresh.astype(jnp.float32)
                for i in range(step):
                    fresh = fresh - coefs[i] * seg[i, j].astype(jnp.float32)
                fresh = (fresh * scale).astype(jnp.bfloat16)
            seg[step, j] = fresh
        theirs = seg[step].reshape((n - 1) * cls, width)

        def total_of(r):
            return (work[r] + dot(dense[r, :, owned * cls:], theirs)).astype(jnp.bfloat16)

        if final:
            each = owned // ncol
            first = [(c, i, lax.rem(mycol + c, ncol) * each + i) for c in range(1, ncol) for i in range(each)]
            for c, i, r in first:
                parts[step, r, mycol] = total_of(r)
                send(parts.at[step, r, mycol], parts.at[step, r, mycol],
                     part_s.at[step, i, c - 1], part_r.at[step, i, ncol - c - 1], 0, c)
            held = [mycol * each + i for i in range(each)]
            for r in held:
                parts[step, r, mycol] = total_of(r)
        else:
            held = list(range(owned))
            for r in held:
                parts[step, r, mycol] = total_of(r)
                for c in range(1, ncol):
                    send(parts.at[step, r, mycol], parts.at[step, r, mycol],
                         part_s.at[step, r, c - 1], part_r.at[step, r, ncol - c - 1], 0, c)
        count = step + 1
        sums = [0.0] * (2 * count + 1)
        for r in held:
            newest = current[r].astype(jnp.float32)
            for i in range(count):
                other = newest if i == step else member(i)[r].astype(jnp.float32)
                sums[count + 1 + i] += jnp.sum(newest * other, axis=0, keepdims=True)
        for i, r in enumerate(held):
            for c in range(1, ncol):
                arrived(parts.at[step, r, lax.rem(mycol + c, ncol)], part_r.at[step, i, c - 1])
            total = diagonal[pl.ds(pl.multiple_of(r * cls, cls), cls), :] * current[r].astype(jnp.float32)
            for k in range(ncol):
                total = total + parts[step, r, k].astype(jnp.float32)
            work[r] = total
            if not final:
                share_coef(step + 1, r, total)
            for i in range(count):
                sums[i] += jnp.sum(total * member(i)[r].astype(jnp.float32), axis=0, keepdims=True)
            sums[count] += jnp.sum(total * total, axis=0, keepdims=True)
        pad = [jnp.zeros((1, width), jnp.float32)] * (8 - len(sums))
        slot = me * ncol + mycol if final else me
        dots[step, slot] = jnp.concatenate(sums + pad, axis=0)
        peers = everyone if final else [(j, 0) for j in range(1, n)]
        for j, c in peers:
            send(dots.at[step, slot], dots.at[step, slot], dot_s.at[step, j, c],
                 dot_r.at[step, (n - j) % n, (ncol - c) % ncol], j, c)
        if not final:
            share_segments(step + 1, work)
        for j, c in peers:
            theirs_at = lax.rem(me + j, n)
            if final:
                theirs_at = theirs_at * ncol + lax.rem(mycol + c, ncol)
            arrived(dots.at[step, theirs_at], dot_r.at[step, j, c])
        total = dots[step, 0]
        for k in range(1, n * ncol if final else n):
            total = total + dots[step, k]
        total = total / panels
        coefs = [total[i:i + 1] for i in range(count)]
        for i in range(count):
            gram[i, step] = gram[step, i] = total[count + 1 + i:count + 2 + i]
        square = total[count:count + 1]
        for i in range(count):
            inner = -2.0 * coefs[i]
            for k in range(count):
                inner = inner + coefs[k] * gram[i, k]
            square = square + coefs[i] * inner
        beta = jnp.sqrt(jnp.maximum(square, 0.0) + 1e-06)
        scale = 1.0 / beta
        if not final:
            pass_on(step + 1)
        for value in coefs + [beta]:
            hess_ref[line:line + 1, :] = value
            line += 1
        for i, r in enumerate(held):
            fresh = work[r]
            for k in range(count):
                fresh = fresh - coefs[k] * member(k)[r].astype(jnp.float32)
            fresh = (fresh * scale).astype(jnp.bfloat16)
            if final:
                last_ref[i * cls:(i + 1) * cls] = fresh
            else:
                basis[step, r] = fresh
    for copy in pending:
        copy.wait_send()


def on_device(vector, self_term, near_blocks, near_rows, near_source, send_index, source_basis,
              target_basis, couplings, far_rows, far_cols):
    owned, rank, cls = source_basis.shape
    width = vector.shape[1]
    n = lax.axis_size("blk")
    ncol = lax.axis_size("col")
    count, links = near_blocks.shape[0], couplings.shape[0]
    block = owned * rank
    share = cls // ncol
    bf16, f32 = jnp.bfloat16, jnp.float32
    vmem, smem = pl.BlockSpec(memory_space=pltpu.VMEM), pl.BlockSpec(memory_space=pltpu.SMEM)
    hbm = pl.BlockSpec(memory_space=pl.ANY)
    dma = pltpu.SemaphoreType.DMA
    return pl.pallas_call(
        functools.partial(solve_kernel, n, ncol),
        out_shape=(
            jax.ShapeDtypeStruct((owned * cls // ncol, width), bf16),
            jax.ShapeDtypeStruct((ITERS * (ITERS + 3) // 2, width), f32),
        ),
        in_specs=[smem] * 5 + [hbm] + [vmem] * 5,
        out_specs=(vmem, vmem),
        scratch_shapes=[
            pltpu.VMEM((count + 1, cls, cls), bf16),
            pltpu.SMEM((count,), jnp.int32),
            pltpu.VMEM((rank, links, rank), f32),
            pltpu.VMEM((owned, cls, (owned + n - 1) * cls), bf16),
            pltpu.VMEM((block, links * rank), bf16),
            pltpu.VMEM((owned, cls, rank), bf16),
            pltpu.VMEM((owned * cls, width), f32),
            pltpu.VMEM((ITERS - 1, owned, cls, width), bf16),
            pltpu.VMEM((owned, cls, width), f32),
            pltpu.VMEM((ITERS, n - 1, share, width), bf16),
            pltpu.VMEM((ITERS, n - 1, ncol, share, width), bf16),
            pltpu.VMEM((ITERS, n - 1, cls, width), bf16),
            pltpu.VMEM((ITERS, n * owned, rank, width), bf16),
            pltpu.VMEM((ITERS, n * owned, rank, width), bf16),
            pltpu.VMEM((links * rank, width), bf16),
            pltpu.VMEM((ITERS, owned, ncol, cls, width), bf16),
            pltpu.VMEM((ITERS, n * ncol, 8, width), f32),
            dma,
            dma((ITERS, n - 1)), dma((ITERS, n - 1)),
            dma((ITERS, n - 1, ncol - 1)), dma((ITERS, n - 1, ncol - 1)),
            dma((ITERS, owned, n - 1)), dma((ITERS, owned, n - 1)),
            dma((ITERS, owned, ncol - 1)), dma((ITERS, owned, ncol - 1)),
            dma((ITERS, n, ncol)), dma((ITERS, n, ncol)),
        ],
        compiler_params=pltpu.CompilerParams(collective_id=0, has_side_effects=True, vmem_limit_bytes=59 << 20),
        name="solve",
    )(near_rows, near_source, send_index, far_rows, far_cols, near_blocks,
      vector.reshape(owned, cls, width), self_term.reshape(-1, 128), source_basis, target_basis,
      couplings.transpose(1, 2, 0))


def solution(mesh):
    placed = (
        P(("grp", "blk"), "rhs"),
        P(("grp", "blk")),
        P(("grp", "blk", "col"), None, None),
        P(("grp", "blk", "col")),
        P(("grp", "blk", "col")),
        P(("grp", "blk"), None),
        P(("grp", "blk"), None, None),
        P(("grp", "blk"), None, None),
        P(("grp", "blk", "col"), None, None),
        P(("grp", "blk", "col")),
        P(("grp", "blk", "col")),
    )
    return jax.shard_map(
        on_device,
        mesh=mesh,
        in_specs=placed,
        out_specs=(P(("grp", "blk", "col"), "rhs"), P("grp", "rhs")),
        check_vma=False,
    )
```

```python
import functools

import jax
import jax.numpy as jnp
from jax import lax
from jax.experimental import pallas as pl
from jax.experimental.pallas import tpu as pltpu
from jax.sharding import PartitionSpec as P

ITERS = 3
MESH = pl.DeviceIdType.MESH


def dot(a, b):
    return jnp.dot(a, b, preferred_element_type=jnp.float32)


def pack(n, rows, cols, near_in, coup_ref, frows_ref, target_ref, self_ref, cells, keys, turned, dense, far, lift,
         diagonal, near_sem, between):
    me = lax.axis_index("blk")
    count, cls, _ = near_in.shape
    owned = target_ref.shape[0]
    rank = turned.shape[0]
    sources = owned + n - 1
    fetch = pltpu.make_async_copy(near_in, cells.at[pl.ds(0, count)], near_sem)
    fetch.start()
    cells[count] = jnp.zeros((cls, cls), jnp.bfloat16)
    for b in range(count):
        source = cols[b]
        place = jnp.where(source < owned, source, owned - 1 + lax.rem(source - owned - me + n, n))
        keys[b] = rows[b] * sources + place

    for k in range(rank):
        turned[k] = coup_ref[k].astype(jnp.float32).T
    per = 128 // rank
    lane = lax.broadcasted_iota(jnp.int32, (rank, 128), 1)
    for g in range(frows_ref.shape[0] // per):
        wide = jnp.concatenate([turned[:, g * per + i, :] for i in range(per)], axis=1)
        row = jnp.full((rank, 128), frows_ref[g * per], jnp.int32)
        for i in range(1, per):
            row = jnp.where(lane >= i * rank, frows_ref[g * per + i], row)
        for r in range(owned):
            far[r * rank:(r + 1) * rank, g * 128:(g + 1) * 128] = jnp.where(row == r, wide, 0.0).astype(jnp.bfloat16)
    for r in range(owned):
        lift[r] = target_ref[r].astype(jnp.float32).T.astype(jnp.bfloat16)

    def latest(key, limit):
        found = jnp.int32(count)
        for b in range(count):
            hit = keys[b] == key
            if limit is not None:
                hit = jnp.logical_and(hit, b < limit)
            found = jnp.where(hit, b, found)
        return found

    for i in range(self_ref.shape[0]):
        column = jnp.broadcast_to(self_ref[i:i + 1], (diagonal.shape[1], 128)).T
        diagonal[i * 128:(i + 1) * 128] = column
    between()
    fetch.wait()

    @pl.loop(0, count)
    def _(b):
        cells[b] = cells[b] + cells[latest(keys[b], b)]

    @pl.loop(0, owned)
    def _(r):
        for c in range(sources):
            dense[r, :, c * cls:(c + 1) * cls] = cells[latest(r * sources + c, None)]


def solve_kernel(n, ncol, rows, cols, send_ref, frows_ref, fcols_ref, near_in, vector_ref, self_ref,
                 source_ref, target_ref, coup_ref,
                 last_ref, hess_ref,
                 cells, keys, turned, dense, far, lift, diagonal,
                 basis, work, outgoing, incoming, seg, raw, coef, chosen, parts, dots,
                 near_sem, out_s, in_r, fwd_s, fwd_r, coef_s, coef_r, part_s, part_r, dot_s, dot_r):
    me = lax.axis_index("blk")
    mycol = lax.axis_index("col")
    owned, cls, width = vector_ref.shape
    rank = source_ref.shape[1]
    panels = n * owned * cls
    block = owned * rank
    share = cls // ncol
    everyone = [(j, c) for j in range(n) for c in range(ncol) if j or c]
    barrier = pltpu.get_barrier_semaphore()

    def at(j, c):
        return {"blk": lax.rem(me + j, n), "col": lax.rem(mycol + c, ncol)}

    for j, c in everyone:
        pl.semaphore_signal(barrier, inc=1, device_id=at(j, c), device_id_type=MESH)
    pl.semaphore_wait(barrier, len(everyone))

    pending = []
    gram = {}
    line = 0

    def member(i):
        return vector_ref if i == 0 else basis.at[i - 1]

    def send(src, dst, ssem, rsem, j, c):
        copy = pltpu.make_async_remote_copy(src_ref=src, dst_ref=dst, send_sem=ssem, recv_sem=rsem,
                                            device_id=at(j, c), device_id_type=MESH)
        copy.start()
        pending.append(copy)

    def arrived(dst, rsem):
        pltpu.make_async_copy(dst, dst, rsem).wait()

    def share_coef(step, c, field):
        mine = raw.at[step, me * owned + c]
        mine[...] = dot(source_ref[c], field.astype(jnp.bfloat16)).astype(jnp.bfloat16)
        for j in range(1, n):
            send(mine, mine, coef_s.at[step, c, j - 1], coef_r.at[step, c, n - j - 1], j, 0)

    def share_segments(step, field):
        for j in range(1, n):
            pick = jnp.minimum(send_ref[0, lax.rem(me + j, n)], owned - 1)
            if step:
                outgoing[step, j - 1] = field[pick].astype(jnp.bfloat16).reshape(ncol, share, width)
                send(outgoing.at[step, j - 1], incoming.at[step, n - j - 1],
                     out_s.at[step, j - 1], in_r.at[step, n - j - 1], j, 0)
                continue
            part = field[pick, pl.ds(pl.multiple_of(mycol * share, share), share), :]
            outgoing[step, j - 1, 0] = part.astype(jnp.bfloat16)
            send(outgoing.at[step, j - 1, 0], incoming.at[step, n - j - 1, mycol],
                 out_s.at[step, j - 1], in_r.at[step, n - j - 1], j, 0)

    def pass_on(step):
        for j in range(1, n):
            here = incoming.at[step, j - 1, mycol]
            arrived(here, in_r.at[step, j - 1])
            for c in range(1, ncol):
                send(here, here, fwd_s.at[step, j - 1, c - 1], fwd_r.at[step, j - 1, ncol - c - 1], 0, c)

    def collect(step):
        for j in range(1, n):
            if step:
                arrived(incoming.at[step, j - 1], in_r.at[step, j - 1])
                continue
            for c in range(1, ncol):
                arrived(incoming.at[step, j - 1, lax.rem(mycol + c, ncol)], fwd_r.at[step, j - 1, c - 1])

    def collect_coefs(step):
        for c in range(owned):
            for j in range(1, n):
                arrived(raw.at[step, lax.rem(me + j, n) * owned + c], coef_r.at[step, c, j - 1])

    share_segments(0, vector_ref)
    for c in range(owned):
        share_coef(0, c, vector_ref[c])
    pack(n, rows, cols, near_in, coup_ref, frows_ref, target_ref, self_ref, cells, keys, turned, dense, far, lift,
         diagonal, near_sem, lambda: pass_on(0))
    coefs, scale = [], None
    for step in range(ITERS):
        current = member(step)
        final = step == ITERS - 1
        mine = current[...].reshape(owned * cls, width)
        for r in range(owned):
            work[r] = dot(dense[r, :, :owned * cls], mine)
        collect_coefs(step)
        fresh = raw[step]
        if step:
            fresh = fresh.astype(jnp.float32)
            for i in range(step):
                fresh = fresh - coefs[i] * coef[i].astype(jnp.float32)
            fresh = (fresh * scale).astype(jnp.bfloat16)
        coef[step] = fresh
        for f in range(fcols_ref.shape[0]):
            chosen[f * rank:(f + 1) * rank] = coef[step, fcols_ref[f]]
        zeta = dot(far[...], chosen[...]).astype(jnp.bfloat16)
        for r in range(owned):
            work[r] += dot(lift[r], zeta[r * rank:(r + 1) * rank])
        collect(step)
        for j in range(n - 1):
            fresh = incoming[step, j].reshape(cls, width)
            if step:
                fresh = fresh.astype(jnp.float32)
                for i in range(step):
                    fresh = fresh - coefs[i] * seg[i, j].astype(jnp.float32)
                fresh = (fresh * scale).astype(jnp.bfloat16)
            seg[step, j] = fresh
        theirs = seg[step].reshape((n - 1) * cls, width)

        def total_of(r):
            return (work[r] + dot(dense[r, :, owned * cls:], theirs)).astype(jnp.bfloat16)

        if final:
            each = owned // ncol
            first = [(c, i, lax.rem(mycol + c, ncol) * each + i) for c in range(1, ncol) for i in range(each)]
            for c, i, r in first:
                parts[step, r, mycol] = total_of(r)
                send(parts.at[step, r, mycol], parts.at[step, r, mycol],
                     part_s.at[step, i, c - 1], part_r.at[step, i, ncol - c - 1], 0, c)
            held = [mycol * each + i for i in range(each)]
            for r in held:
                parts[step, r, mycol] = total_of(r)
        else:
            held = list(range(owned))
            for r in held:
                parts[step, r, mycol] = total_of(r)
                for c in range(1, ncol):
                    send(parts.at[step, r, mycol], parts.at[step, r, mycol],
                         part_s.at[step, r, c - 1], part_r.at[step, r, ncol - c - 1], 0, c)
        count = step + 1
        sums = [0.0] * (2 * count + 1)
        for r in held:
            newest = current[r].astype(jnp.float32)
            for i in range(count):
                other = newest if i == step else member(i)[r].astype(jnp.float32)
                sums[count + 1 + i] += jnp.sum(newest * other, axis=0, keepdims=True)
        for i, r in enumerate(held):
            for c in range(1, ncol):
                arrived(parts.at[step, r, lax.rem(mycol + c, ncol)], part_r.at[step, i, c - 1])
            total = diagonal[pl.ds(pl.multiple_of(r * cls, cls), cls), :] * current[r].astype(jnp.float32)
            for k in range(ncol):
                total = total + parts[step, r, k].astype(jnp.float32)
            work[r] = total
            if not final:
                share_coef(step + 1, r, total)
            for i in range(count):
                sums[i] += jnp.sum(total * member(i)[r].astype(jnp.float32), axis=0, keepdims=True)
            sums[count] += jnp.sum(total * total, axis=0, keepdims=True)
        pad = [jnp.zeros((1, width), jnp.float32)] * (8 - len(sums))
        slot = me * ncol + mycol if final else me
        dots[step, slot] = jnp.concatenate(sums + pad, axis=0)
        peers = everyone if final else [(j, 0) for j in range(1, n)]
        for j, c in peers:
            send(dots.at[step, slot], dots.at[step, slot], dot_s.at[step, j, c],
                 dot_r.at[step, (n - j) % n, (ncol - c) % ncol], j, c)
        if not final:
            share_segments(step + 1, work)
        for j, c in peers:
            theirs_at = lax.rem(me + j, n)
            if final:
                theirs_at = theirs_at * ncol + lax.rem(mycol + c, ncol)
            arrived(dots.at[step, theirs_at], dot_r.at[step, j, c])
        total = dots[step, 0]
        for k in range(1, n * ncol if final else n):
            total = total + dots[step, k]
        total = total / panels
        coefs = [total[i:i + 1] for i in range(count)]
        for i in range(count):
            gram[i, step] = gram[step, i] = total[count + 1 + i:count + 2 + i]
        square = total[count:count + 1]
        for i in range(count):
            inner = -2.0 * coefs[i]
            for k in range(count):
                inner = inner + coefs[k] * gram[i, k]
            square = square + coefs[i] * inner
        beta = jnp.sqrt(jnp.maximum(square, 0.0) + 1e-06)
        scale = 1.0 / beta
        for value in coefs + [beta]:
            hess_ref[line:line + 1, :] = value
            line += 1
        for i, r in enumerate(held):
            fresh = work[r]
            for k in range(count):
                fresh = fresh - coefs[k] * member(k)[r].astype(jnp.float32)
            fresh = (fresh * scale).astype(jnp.bfloat16)
            if final:
                last_ref[i * cls:(i + 1) * cls] = fresh
            else:
                basis[step, r] = fresh
    for copy in pending:
        copy.wait_send()


def on_device(vector, self_term, near_blocks, near_rows, near_source, send_index, source_basis,
              target_basis, couplings, far_rows, far_cols):
    owned, rank, cls = source_basis.shape
    width = vector.shape[1]
    n = lax.axis_size("blk")
    ncol = lax.axis_size("col")
    count, links = near_blocks.shape[0], couplings.shape[0]
    block = owned * rank
    share = cls // ncol
    bf16, f32 = jnp.bfloat16, jnp.float32
    vmem, smem = pl.BlockSpec(memory_space=pltpu.VMEM), pl.BlockSpec(memory_space=pltpu.SMEM)
    hbm = pl.BlockSpec(memory_space=pltpu.HBM)
    dma = pltpu.SemaphoreType.DMA
    return pl.pallas_call(
        functools.partial(solve_kernel, n, ncol),
        out_shape=(
            jax.ShapeDtypeStruct((owned * cls // ncol, width), bf16),
            jax.ShapeDtypeStruct((ITERS * (ITERS + 3) // 2, width), f32),
        ),
        in_specs=[smem] * 5 + [hbm] + [vmem] * 5,
        out_specs=(vmem, vmem),
        scratch_shapes=[
            pltpu.VMEM((count + 1, cls, cls), bf16),
            pltpu.SMEM((count,), jnp.int32),
            pltpu.VMEM((rank, links, rank), f32),
            pltpu.VMEM((owned, cls, (owned + n - 1) * cls), bf16),
            pltpu.VMEM((block, links * rank), bf16),
            pltpu.VMEM((owned, cls, rank), bf16),
            pltpu.VMEM((owned * cls, width), f32),
            pltpu.VMEM((ITERS - 1, owned, cls, width), bf16),
            pltpu.VMEM((owned, cls, width), f32),
            pltpu.VMEM((ITERS, n - 1, ncol, share, width), bf16),
            pltpu.VMEM((ITERS, n - 1, ncol, share, width), bf16),
            pltpu.VMEM((ITERS, n - 1, cls, width), bf16),
            pltpu.VMEM((ITERS, n * owned, rank, width), bf16),
            pltpu.VMEM((ITERS, n * owned, rank, width), bf16),
            pltpu.VMEM((links * rank, width), bf16),
            pltpu.VMEM((ITERS, owned, ncol, cls, width), bf16),
            pltpu.VMEM((ITERS, n * ncol, 8, width), f32),
            dma,
            dma((ITERS, n - 1)), dma((ITERS, n - 1)),
            dma((ITERS, n - 1, ncol - 1)), dma((ITERS, n - 1, ncol - 1)),
            dma((ITERS, owned, n - 1)), dma((ITERS, owned, n - 1)),
            dma((ITERS, owned, ncol - 1)), dma((ITERS, owned, ncol - 1)),
            dma((ITERS, n, ncol)), dma((ITERS, n, ncol)),
        ],
        compiler_params=pltpu.CompilerParams(collective_id=0, has_side_effects=True, vmem_limit_bytes=60 << 20),
        name="solve",
    )(near_rows, near_source, send_index, far_rows, far_cols, near_blocks,
      vector.reshape(owned, cls, width), self_term.reshape(-1, 128), source_basis, target_basis,
      couplings.transpose(1, 2, 0))


def solution(mesh):
    placed = (
        P(("grp", "blk"), "rhs"),
        P(("grp", "blk")),
        P(("grp", "blk", "col"), None, None),
        P(("grp", "blk", "col")),
        P(("grp", "blk", "col")),
        P(("grp", "blk"), None),
        P(("grp", "blk"), None, None),
        P(("grp", "blk"), None, None),
        P(("grp", "blk", "col"), None, None),
        P(("grp", "blk", "col")),
        P(("grp", "blk", "col")),
    )
    return jax.shard_map(
        on_device,
        mesh=mesh,
        in_specs=placed,
        out_specs=(P(("grp", "blk", "col"), "rhs"), P("grp", "rhs")),
        check_vma=False,
    )
```
